32 devices in a mesh: dp: 8 (over z, core), expert: 4 (over y, x).
Axes of the slice: x: 2, y: 2, z: 4, core: 2. Of those that a mesh axis runs over, the one named last changes fastest.
Arguments:
- hidden_in: bfloat16 [2048, 2048], P(('dp', 'expert')), parts along dimension 0, may hold values from -6 to 6
- route_ids: int32 [2048, 2], P(('dp', 'expert')), parts along dimension 0, may hold values from 0 to 3, all different within a row; in each aligned block of 64 rows (0 to 63, 64 to 127, ...) at most 64 rows name the same one
- gates: float32 [2048, 2], P(('dp', 'expert')), parts along dimension 0, may hold values from 0.05 to 1
- w_in: bfloat16 [4, 2048, 1536], P('expert'), may hold values from -0.125 to 0.125
- w_out: bfloat16 [4, 768, 2048], P('expert'), may hold values from -0.21875 to 0.21875
Outputs:
- combined: bfloat16 [2048, 2048], P(('dp', 'expert')), parts along dimension 0
The draws below stay inside these ranges and needn't reach their ends.
There are 8 independent parts, one for each index of `dp`. The reference program is written for one: setup_inputs(seed, part) draws one part's arguments, and reference() takes and returns one part's arrays. A program takes and returns all parts, laid end to end along the dimension named above; an argument that names none is the same for every part. Nothing has to cross between parts.
Inputs may be any that keep to these rules, and one draw needn't show every extreme that they name: `route_ids`: each row names 2 different experts. Among the rows of one device (aligned blocks of 64 rows) no expert is named by more than 64 rows, and in every draw some expert is named by exactly 64 rows of some block.
All inputs are finite; a program needn't handle non-finite values.
Results may differ from the reference program's by a relative error of at most 0.0085.
Values may be sent and summed in bfloat16 or wider, within the bound.
A program may use at most 64 MiB of HBM per device.

```python
import math
import jax
import jax.numpy as jnp
import numpy as np
from jax import lax

D = 2048
FF = 768
ROWS_DEV = 64
EXPERTS = 4
TOP = 2
CAP = 64
ROWS = 256


def block_levels(own_key, shape, shards, least, top_value):
    def one(dim, blocks):
        heights = jax.random.uniform(jax.random.fold_in(jax.random.fold_in(own_key, 6), dim), (blocks,), jnp.float32, least / len(shards), top_value / len(shards))
        return jnp.repeat(jnp.exp(heights), shape[dim] // blocks).reshape((-1,) + (1,) * (len(shape) - dim - 1))

    factor_of = one(*shards[0])
    for cut in shards[1:]:
        factor_of = factor_of * one(*cut)
    return factor_of


def shared_out(rng, own, number, rows, count, top, limit, skew):
    order = jax.random.permutation(rng, count)
    packed, ordinary = portions_of(count, rows * top, limit, skew, True), portions_of(count, rows * top, limit, skew, False)
    places = jnp.arange(count)

    def named(sizes, offset_by):
        used = int((sizes > 0).sum())
        fixed = max(1, used // 4)
        shifted = fixed + (places - fixed + offset_by * (used - fixed)) % max(1, count - fixed)
        return jnp.zeros((count,), jnp.int32).at[order[jnp.where(places < fixed, places, shifted)]].set(jnp.asarray(sizes, jnp.int32))

    sizes = jnp.where(number % 4 == 0, named(packed, number // 4), named(ordinary, number - number // 4 - 1))
    mixed = jax.random.permutation(jax.random.fold_in(own, 3), count)
    giver, sink = mixed[0:count // 2 * 2:2], mixed[1:count // 2 * 2:2]
    slack = jnp.minimum(sizes[giver] - 1, limit - sizes[sink]) // 2
    slack = jnp.where((giver == order[0]) | (sink == order[0]) | (sizes[sink] == 0), 0, jnp.maximum(slack, 0))
    shifted = jax.random.randint(jax.random.fold_in(own, 4), (count // 2,), 0, 1 << 20) % (slack + 1)
    sizes = sizes.at[giver].add(-shifted).at[sink].add(shifted)
    members = jnp.searchsorted(jnp.cumsum(sizes), jnp.arange(rows * top), side="right").astype(jnp.int32)
    grid = members.reshape(top, rows).T
    grid = grid[jax.random.permutation(jax.random.fold_in(own, 1), rows)]
    offset_by = jax.random.randint(jax.random.fold_in(own, 2), (rows, 1), 0, top)
    return jnp.take_along_axis(grid, (jnp.arange(top)[None, :] + offset_by) % top, axis=1)


def portions_of(number_of, total, reach, slope, full):
    loads = [(1 << 20) // math.isqrt(standing ** slope) + 1 for standing in range(1, number_of + 1)]
    largest = reach if full else min(reach, max(-(-total // number_of), total * loads[0] // sum(loads)))
    least = 1 if total - largest >= number_of - 1 else 0
    given, rest = [largest] + [least] * (number_of - 1), total - largest - least * (number_of - 1)
    while rest > 0:
        free = [i for i in range(1, number_of) if given[i] < largest] or [i for i in range(1, number_of) if given[i] < reach]
        mass, left = sum([loads[i] for i in free]), rest
        for i in free:
            more = min(reach - given[i], max(1, left * loads[i] // mass), rest)
            given[i] = given[i] + more
            rest = rest - more
    return np.array(given)


def noise(stream_key, shape, scale, most, pieces=(), kind=jnp.bfloat16):
    array = jax.random.normal(stream_key, shape, jnp.float32) * scale
    if len(pieces) > 0:
        array = block_levels(stream_key, shape, pieces, -0.22, 0.18) * array
    return jnp.clip(array, min=-most, max=most).astype(kind)


def setup_inputs(seed: int = 0, part: int = 0) -> dict:
    keys = jax.random.split(jax.random.key(seed), 6)
    part_splits = jax.random.split(jax.random.fold_in(keys[5], part), 6)
    hidden_in = noise(part_splits[0], (ROWS, D), 1.0, 6.0, ((0, 4),))
    route_ids_keys = jax.random.split(jax.random.fold_in(part_splits[1], 1), ROWS // ROWS_DEV)
    route_ids_turns = jax.random.permutation(jax.random.fold_in(part_splits[1], 3), ROWS // ROWS_DEV)
    route_ids = jax.vmap(lambda own, number: shared_out(jax.random.fold_in(part_splits[1], 2), own, number, ROWS_DEV, EXPERTS, TOP, CAP, 2))(route_ids_keys, route_ids_turns).reshape((ROWS, TOP))
    gates = jnp.clip(jnp.exp(math.log(1.0) - 2.9957323 * jax.random.uniform(part_splits[2], (ROWS, TOP), jnp.float32) ** block_levels(part_splits[2], (ROWS, TOP), ((0, 4),), -0.2, 0.2)), 0.05, 1.0)
    w_in = noise(keys[3], (EXPERTS, D, 2 * FF), D ** -0.5, 0.125, ((0, 4),))
    w_out = noise(keys[4], (EXPERTS, FF, D), FF ** -0.5, 0.21875, ((0, 4),))
    return dict(hidden_in=hidden_in, route_ids=route_ids, gates=gates, w_in=w_in, w_out=w_out)


def reference(hidden_in, route_ids, gates, w_in, w_out):
    def one_expert(carry, expert_id):
        weight_row = jnp.sum(jnp.where(route_ids == expert_id, gates, jnp.float32(0.0)), axis=1)
        projected = jnp.dot(hidden_in, w_in[expert_id], preferred_element_type=jnp.float32)
        inner = (jax.nn.silu(projected[:, :FF]) * projected[:, FF:]).astype(jnp.bfloat16)
        result = jnp.dot(inner, w_out[expert_id], preferred_element_type=jnp.float32).astype(jnp.bfloat16)
        return carry + weight_row[:, None] * result.astype(jnp.float32), None

    start = jnp.zeros((hidden_in.shape[0], D), jnp.float32)
    total, unused = lax.scan(one_expert, start, jnp.arange(EXPERTS, dtype=jnp.int32))
    return total.astype(jnp.bfloat16)
```

```python
import jax
import jax.numpy as jnp
from jax import lax
from jax.experimental import pallas as pl
from jax.experimental.pallas import tpu as pltpu
from jax.sharding import PartitionSpec as P


def slot_ranks(choices, count):
    flat = choices.reshape(choices.shape[:-2] + (-1,))
    length = flat.shape[-1]
    onehot = (flat[..., None] == jnp.arange(count, dtype=jnp.int32)).astype(jnp.bfloat16)
    lower = (
        jnp.arange(length, dtype=jnp.int32)[:, None] > jnp.arange(length, dtype=jnp.int32)[None, :]
    ).astype(jnp.bfloat16)
    ranks = jnp.einsum("ij,...jn->...in", lower, onehot, preferred_element_type=jnp.float32)
    picked = jnp.sum(ranks * onehot.astype(jnp.float32), axis=-1)
    return picked.astype(jnp.int32).reshape(choices.shape)


def body(hidden_in, route_ids, gates, w_in, w_out):
    groups = lax.axis_size("expert")
    rows_here = hidden_in.shape[0]
    capacity = 2 * rows_here * route_ids.shape[1] // groups
    width = hidden_in.shape[1]
    half = w_out.shape[1]
    slots_all = capacity * groups
    slot_of = slot_ranks(route_ids, groups)
    place_key = slot_of * groups + route_ids
    key_table = (place_key[:, :, None] == jnp.arange(slots_all, dtype=jnp.int32)).astype(
        jnp.float32
    )
    placement = jnp.sum(key_table, axis=1).astype(jnp.bfloat16)
    outgoing = jnp.einsum("rs,rd->sd", placement, hidden_in, preferred_element_type=jnp.float32)
    outgoing = outgoing.astype(jnp.bfloat16).reshape(capacity, groups, width)
    projected = jnp.einsum(
        "cnd,df->cnf",
        lax.all_to_all(outgoing, "expert", split_axis=1, concat_axis=1, tiled=True),
        w_in[0],
        preferred_element_type=jnp.float32,
    )
    inner = (jax.nn.silu(projected[..., :half]) * projected[..., half:]).astype(jnp.bfloat16)
    produced = jnp.einsum(
        "cnf,fd->cnd", inner, w_out[0], preferred_element_type=jnp.float32
    ).astype(jnp.bfloat16)
    returned = lax.all_to_all(produced, "expert", split_axis=1, concat_axis=1, tiled=True)
    weighting = jnp.sum(gates[:, :, None] * key_table, axis=1)
    total = jnp.dot(
        weighting,
        returned.reshape(slots_all, width).astype(jnp.float32),
        precision=lax.Precision.HIGHEST,
    )
    return total.astype(jnp.bfloat16)

CHUNKS = 2
X, Y, DIAG = 1, 2, 3


def quad_kernel(
    ids_ref, gates_ref, hidden_ref, w_in_ref, w_out_ref, out_ref,
    win, wout, rows, inner, sums, table, via_x, via_y, fin_x, fin_y,
    load_sem, table_send, table_recv, go_send, go_recv, back_send, back_recv,
):
    me = lax.axis_index("expert")
    x_bit = lax.rem(me, 2)
    y_bit = me // 2
    ids_of = [me, 2 * y_bit + 1 - x_bit, 2 * (1 - y_bit) + x_bit, 3 - me]
    total_rows, width = hidden_ref.shape
    step = total_rows // CHUNKS
    hw = width // 2
    half = wout.shape[0]
    left, right = pl.ds(0, hw), pl.ds(hw, hw)

    def remote(src, dst, send, recv, to):
        return pltpu.make_async_remote_copy(
            src_ref=src, dst_ref=dst, send_sem=send, recv_sem=recv,
            device_id={"expert": ids_of[to]}, device_id_type=pl.DeviceIdType.MESH,
        )

    own = [
        pltpu.make_async_copy(
            hidden_ref.at[pl.ds(c * step, step)], rows.at[c, 0], load_sem.at[c]
        )
        for c in range(CHUNKS)
    ]
    for copy in own:
        copy.start()
    load_in = pltpu.make_async_copy(w_in_ref.at[0], win, load_sem.at[CHUNKS])
    load_out = pltpu.make_async_copy(w_out_ref.at[0], wout, load_sem.at[CHUNKS + 1])
    load_in.start()
    load_out.start()

    barrier = pltpu.get_barrier_semaphore()
    for s in (X, Y, DIAG):
        pl.semaphore_signal(
            barrier, inc=1, device_id={"expert": ids_of[s]}, device_id_type=pl.DeviceIdType.MESH
        )

    for s in range(4):
        line = jnp.sum(
            jnp.where(ids_ref[...] == ids_of[s], gates_ref[...], jnp.float32(0.0)),
            axis=0, keepdims=True,
        )
        tile = 0 if s == 0 else 3 + s
        table[tile] = jnp.zeros_like(table[tile])
        table[tile, :, :total_rows] = jnp.broadcast_to(line, (8, total_rows))
    pl.semaphore_wait(barrier, 3)

    def go(c, index, src, dst_slot, cols, to):
        return remote(
            src, rows.at[c, dst_slot, :, cols], go_send.at[c, index], go_recv.at[c, index], to
        )

    sent = []
    for c in range(CHUNKS):
        own[c].wait()
        for index, cols, to in ((0, left, X), (1, right, Y), (2, right, X), (3, left, Y)):
            copy = go(c, index, rows.at[c, 0, :, cols], to, cols, to)
            copy.start()
            sent.append(copy)
        if c == 0:
            tables = [
                remote(table.at[3 + s], table.at[s], table_send.at[s - 1], table_recv.at[s - 1], s)
                for s in (X, Y, DIAG)
            ]
            for copy in tables:
                copy.start()

    def forward(c):
        first, second = sent[4 * c], sent[4 * c + 1]
        on_y = go(c, 4, rows.at[c, X, :, left], DIAG, left, Y)
        on_x = go(c, 5, rows.at[c, Y, :, right], DIAG, right, X)
        first.wait_recv()
        on_y.start()
        second.wait_recv()
        on_x.start()
        return on_y, on_x

    forwards = [forward(0)]
    columns = None
    back = []
    for c in range(CHUNKS):
        if c + 1 < CHUNKS:
            forwards.append(forward(c + 1))
        sent[4 * c + 2].wait_recv()
        sent[4 * c + 3].wait_recv()
        if c == 0:
            for copy in tables:
                copy.wait_recv()
            columns = [jnp.transpose(table[s])[:total_rows, 0:1] for s in range(4)]
            load_in.wait()
        for copy in forwards[c]:
            copy.wait_recv()
        x = rows[c].reshape(4 * step, width)
        for f in range(0, half, 256):
            gate = jnp.dot(x, win[:, f : f + 256], preferred_element_type=jnp.float32)
            up = jnp.dot(
                x, win[:, half + f : half + f + 256], preferred_element_type=jnp.float32
            )
            inner[:, f : f + 256] = (gate / (1.0 + jnp.exp(-gate)) * up).astype(inner.dtype)
        if c == 0:
            load_out.wait()
        h = inner[...]
        weight = jnp.concatenate([col[c * step : (c + 1) * step] for col in columns], axis=0)
        for d in range(0, width, 512):
            made = jnp.dot(h, wout[:, d : d + 512], preferred_element_type=jnp.float32)
            sums[c, :, :, d : d + 512] = (
                (made * weight).astype(sums.dtype).reshape(4, step, 512)
            )

        def send(index, src, dst, to):
            copy = remote(src, dst, back_send.at[c, index], back_recv.at[c, index], to)
            copy.start()
            return copy

        back.append([
            send(0, sums.at[c, DIAG, :, left], via_x.at[c], X),
            send(1, sums.at[c, DIAG, :, right], via_y.at[c], Y),
            send(2, sums.at[c, X, :, left], fin_x.at[c, :, left], X),
            send(3, sums.at[c, Y, :, right], fin_y.at[c, :, right], Y),
        ])

    for c in range(CHUNKS):
        def relay(index, came, slot, cols, held, dst):
            came.wait_recv()
            sums[c, slot, :, cols] = (
                sums[c, slot, :, cols].astype(jnp.float32) + held[c].astype(jnp.float32)
            ).astype(sums.dtype)
            copy = remote(
                sums.at[c, slot, :, cols], dst, back_send.at[c, index], back_recv.at[c, index], slot
            )
            copy.start()
            return copy

        back[c].append(relay(4, back[c][0], Y, left, via_x, fin_y.at[c, :, left]))
        back[c].append(relay(5, back[c][1], X, right, via_y, fin_x.at[c, :, right]))

    for c in range(CHUNKS):
        for copy in back[c][2:]:
            copy.wait_recv()
        out_ref[pl.ds(c * step, step), :] = (
            sums[c, 0].astype(jnp.float32)
            + fin_x[c].astype(jnp.float32)
            + fin_y[c].astype(jnp.float32)
        ).astype(out_ref.dtype)

    for copy in sent + tables + [f for pair in forwards for f in pair] + sum(back, []):
        copy.wait_send()


def quad_body(hidden_in, route_ids, gates, w_in, w_out):
    rows, width = hidden_in.shape
    half = w_out.shape[1]
    step = rows // CHUNKS
    kind = hidden_in.dtype
    vmem = pl.BlockSpec(memory_space=pltpu.VMEM)
    anywhere = pl.BlockSpec(memory_space=pl.ANY)
    dma = pltpu.SemaphoreType.DMA
    return pl.pallas_call(
        quad_kernel,
        out_shape=jax.ShapeDtypeStruct((rows, width), kind),
        in_specs=[vmem, vmem, anywhere, anywhere, anywhere],
        out_specs=vmem,
        scratch_shapes=[
            pltpu.VMEM((width, 2 * half), kind),
            pltpu.VMEM((half, width), kind),
            pltpu.VMEM((CHUNKS, 4, step, width), kind),
            pltpu.VMEM((4 * step, half), kind),
            pltpu.VMEM((CHUNKS, 4, step, width), kind),
            pltpu.VMEM((7, 8, 128), jnp.float32),
            pltpu.VMEM((CHUNKS, step, width // 2), kind),
            pltpu.VMEM((CHUNKS, step, width // 2), kind),
            pltpu.VMEM((CHUNKS, step, width), kind),
            pltpu.VMEM((CHUNKS, step, width), kind),
            dma((CHUNKS + 2,)),
            dma((3,)),
            dma((3,)),
            dma((CHUNKS, 6)),
            dma((CHUNKS, 6)),
            dma((CHUNKS, 6)),
            dma((CHUNKS, 6)),
        ],
        compiler_params=pltpu.CompilerParams(
            collective_id=0, has_side_effects=True, vmem_limit_bytes=56 * 1024 * 1024
        ),
    )(route_ids.T, gates.T, hidden_in, w_in, w_out)


def solution(mesh):
    placed = (
        P(("dp", "expert"), None),
        P(("dp", "expert"), None),
        P(("dp", "expert"), None),
        P("expert", None, None),
        P("expert", None, None),
    )
    local = quad_body if mesh.shape["expert"] == 4 else body
    return jax.shard_map(
        local, mesh=mesh, in_specs=placed, out_specs=P(("dp", "expert"), None), check_vma=False
    )
```

```python
import jax
import jax.numpy as jnp
from jax import lax
from jax.experimental import pallas as pl
from jax.experimental.pallas import tpu as pltpu
from jax.sharding import PartitionSpec as P


def slot_ranks(choices, count):
    flat = choices.reshape(choices.shape[:-2] + (-1,))
    length = flat.shape[-1]
    onehot = (flat[..., None] == jnp.arange(count, dtype=jnp.int32)).astype(jnp.bfloat16)
    lower = (
        jnp.arange(length, dtype=jnp.int32)[:, None] > jnp.arange(length, dtype=jnp.int32)[None, :]
    ).astype(jnp.bfloat16)
    ranks = jnp.einsum("ij,...jn->...in", lower, onehot, preferred_element_type=jnp.float32)
    picked = jnp.sum(ranks * onehot.astype(jnp.float32), axis=-1)
    return picked.astype(jnp.int32).reshape(choices.shape)


def body(hidden_in, route_ids, gates, w_in, w_out):
    groups = lax.axis_size("expert")
    rows_here = hidden_in.shape[0]
    capacity = 2 * rows_here * route_ids.shape[1] // groups
    width = hidden_in.shape[1]
    half = w_out.shape[1]
    slots_all = capacity * groups
    slot_of = slot_ranks(route_ids, groups)
    place_key = slot_of * groups + route_ids
    key_table = (place_key[:, :, None] == jnp.arange(slots_all, dtype=jnp.int32)).astype(
        jnp.float32
    )
    placement = jnp.sum(key_table, axis=1).astype(jnp.bfloat16)
    outgoing = jnp.einsum("rs,rd->sd", placement, hidden_in, preferred_element_type=jnp.float32)
    outgoing = outgoing.astype(jnp.bfloat16).reshape(capacity, groups, width)
    projected = jnp.einsum(
        "cnd,df->cnf",
        lax.all_to_all(outgoing, "expert", split_axis=1, concat_axis=1, tiled=True),
        w_in[0],
        preferred_element_type=jnp.float32,
    )
    inner = (jax.nn.silu(projected[..., :half]) * projected[..., half:]).astype(jnp.bfloat16)
    produced = jnp.einsum(
        "cnf,fd->cnd", inner, w_out[0], preferred_element_type=jnp.float32
    ).astype(jnp.bfloat16)
    returned = lax.all_to_all(produced, "expert", split_axis=1, concat_axis=1, tiled=True)
    weighting = jnp.sum(gates[:, :, None] * key_table, axis=1)
    total = jnp.dot(
        weighting,
        returned.reshape(slots_all, width).astype(jnp.float32),
        precision=lax.Precision.HIGHEST,
    )
    return total.astype(jnp.bfloat16)

CHUNKS = 2
X, Y, DIAG = 1, 2, 3


def quad_kernel(
    ids_ref, gates_ref, hidden_ref, w_in_ref, w_out_ref, out_ref,
    win, wout, rows, inner, sums, table, via_x, via_y, fin_x, fin_y,
    load_sem, table_send, table_recv, go_send, go_recv, back_send, back_recv,
):
    me = lax.axis_index("expert")
    x_bit = lax.rem(me, 2)
    y_bit = me // 2
    ids_of = [me, 2 * y_bit + 1 - x_bit, 2 * (1 - y_bit) + x_bit, 3 - me]
    total_rows, width = hidden_ref.shape
    step = total_rows // CHUNKS
    part = step // 2
    half = wout.shape[0]
    low, high = pl.ds(0, part), pl.ds(part, part)

    def remote(src, dst, send, recv, to):
        return pltpu.make_async_remote_copy(
            src_ref=src, dst_ref=dst, send_sem=send, recv_sem=recv,
            device_id={"expert": ids_of[to]}, device_id_type=pl.DeviceIdType.MESH,
        )

    own = [
        pltpu.make_async_copy(
            hidden_ref.at[pl.ds(c * step, step)], rows.at[c, 0], load_sem.at[c]
        )
        for c in range(CHUNKS)
    ]
    for copy in own:
        copy.start()
    load_in = pltpu.make_async_copy(w_in_ref.at[0], win, load_sem.at[CHUNKS])
    load_out = pltpu.make_async_copy(w_out_ref.at[0], wout, load_sem.at[CHUNKS + 1])
    load_in.start()
    load_out.start()

    barrier = pltpu.get_barrier_semaphore()
    for s in (X, Y, DIAG):
        pl.semaphore_signal(
            barrier, inc=1, device_id={"expert": ids_of[s]}, device_id_type=pl.DeviceIdType.MESH
        )

    for s in range(4):
        line = jnp.sum(
            jnp.where(ids_ref[...] == ids_of[s], gates_ref[...], jnp.float32(0.0)),
            axis=0, keepdims=True,
        )
        tile = 0 if s == 0 else 3 + s
        table[tile] = jnp.zeros_like(table[tile])
        table[tile, :, :total_rows] = jnp.broadcast_to(line, (8, total_rows))
    pl.semaphore_wait(barrier, 3)

    def go(c, index, src_slot, dst_slot, span, to):
        copy = remote(
            rows.at[c, src_slot, span], rows.at[c, dst_slot, span],
            go_send.at[c, index], go_recv.at[c, index], to,
        )
        copy.start()
        return copy

    def first_half(c):
        own[c].wait()
        return [go(c, 0, 0, X, low, X), go(c, 1, 0, Y, high, Y)]

    def second_half(c):
        return [go(c, 2, 0, X, high, X), go(c, 3, 0, Y, low, Y)]

    def forward(first):
        c, (from_x, from_y) = first
        from_x.wait_recv()
        on_y = go(c, 4, X, DIAG, low, Y)
        from_y.wait_recv()
        return [on_y, go(c, 5, Y, DIAG, high, X)]

    firsts, seconds, forwards = [first_half(0)], [second_half(0)], []
    tables = [
        remote(table.at[3 + s], table.at[s], table_send.at[s - 1], table_recv.at[s - 1], s)
        for s in (X, Y, DIAG)
    ]
    for copy in tables:
        copy.start()
    for c in range(1, CHUNKS):
        firsts.append(first_half(c))
        forwards.append(forward((c - 1, firsts[c - 1])))
        seconds.append(second_half(c))
    forwards.append(forward((CHUNKS - 1, firsts[-1])))
    columns = None
    back = []
    for c in range(CHUNKS):
        for copy in seconds[c]:
            copy.wait_recv()
        if c == 0:
            for copy in tables:
                copy.wait_recv()
            columns = [jnp.transpose(table[s])[:total_rows, 0:1] for s in range(4)]
            load_in.wait()
        for copy in forwards[c]:
            copy.wait_recv()
        x = rows[c].reshape(4 * step, width)
        for f in range(0, half, 256):
            gate = jnp.dot(x, win[:, f : f + 256], preferred_element_type=jnp.float32)
            up = jnp.dot(
                x, win[:, half + f : half + f + 256], preferred_element_type=jnp.float32
            )
            inner[:, f : f + 256] = (gate / (1.0 + jnp.exp(-gate)) * up).astype(inner.dtype)
        if c == 0:
            load_out.wait()
        h = inner[...]
        weight = jnp.concatenate([col[c * step : (c + 1) * step] for col in columns], axis=0)
        for d in range(0, width, 512):
            made = jnp.dot(h, wout[:, d : d + 512], preferred_element_type=jnp.float32)
            sums[c, :, :, d : d + 512] = (
                (made * weight).astype(sums.dtype).reshape(4, step, 512)
            )

        def send(index, src, dst, to):
            copy = remote(src, dst, back_send.at[c, index], back_recv.at[c, index], to)
            copy.start()
            return copy

        back.append([
            send(0, sums.at[c, DIAG, low], via_x.at[c], X),
            send(1, sums.at[c, DIAG, high], via_y.at[c], Y),
            send(2, sums.at[c, X, low], fin_x.at[c, low], X),
            send(3, sums.at[c, Y, high], fin_y.at[c, high], Y),
        ])

    for c in range(CHUNKS):
        def relay(index, came, slot, span, held, dst):
            came.wait_recv()
            sums[c, slot, span] = (
                sums[c, slot, span].astype(jnp.float32) + held[c].astype(jnp.float32)
            ).astype(sums.dtype)
            copy = remote(
                sums.at[c, slot, span], dst, back_send.at[c, index], back_recv.at[c, index], slot
            )
            copy.start()
            return copy

        back[c].append(relay(4, back[c][0], Y, low, via_x, fin_y.at[c, low]))
        back[c].append(relay(5, back[c][1], X, high, via_y, fin_x.at[c, high]))

    for c in range(CHUNKS):
        for copy in back[c][2:]:
            copy.wait_recv()
        out_ref[pl.ds(c * step, step), :] = (
            sums[c, 0].astype(jnp.float32)
            + fin_x[c].astype(jnp.float32)
            + fin_y[c].astype(jnp.float32)
        ).astype(out_ref.dtype)

    for copy in tables + sum(firsts + seconds + forwards + back, []):
        copy.wait_send()


def quad_body(hidden_in, route_ids, gates, w_in, w_out):
    rows, width = hidden_in.shape
    half = w_out.shape[1]
    step = rows // CHUNKS
    kind = hidden_in.dtype
    vmem = pl.BlockSpec(memory_space=pltpu.VMEM)
    anywhere = pl.BlockSpec(memory_space=pl.ANY)
    dma = pltpu.SemaphoreType.DMA
    return pl.pallas_call(
        quad_kernel,
        out_shape=pltpu.VMEM((rows, width), kind),
        in_specs=[vmem, vmem, anywhere, anywhere, anywhere],
        out_specs=vmem,
        scratch_shapes=[
            pltpu.VMEM((width, 2 * half), kind),
            pltpu.VMEM((half, width), kind),
            pltpu.VMEM((CHUNKS, 4, step, width), kind),
            pltpu.VMEM((4 * step, half), kind),
            pltpu.VMEM((CHUNKS, 4, step, width), kind),
            pltpu.VMEM((7, 8, 128), jnp.float32),
            pltpu.VMEM((CHUNKS, step // 2, width), kind),
            pltpu.VMEM((CHUNKS, step // 2, width), kind),
            pltpu.VMEM((CHUNKS, step, width), kind),
            pltpu.VMEM((CHUNKS, step, width), kind),
            dma((CHUNKS + 2,)),
            dma((3,)),
            dma((3,)),
            dma((CHUNKS, 6)),
            dma((CHUNKS, 6)),
            dma((CHUNKS, 6)),
            dma((CHUNKS, 6)),
        ],
        compiler_params=pltpu.CompilerParams(
            collective_id=0, has_side_effects=True, vmem_limit_bytes=56 * 1024 * 1024
        ),
    )(route_ids.T, gates.T, hidden_in, w_in, w_out)


def solution(mesh):
    placed = (
        P(("dp", "expert"), None),
        P(("dp", "expert"), None),
        P(("dp", "expert"), None),
        P("expert", None, None),
        P("expert", None, None),
    )
    local = quad_body if mesh.shape["expert"] == 4 else body
    return jax.shard_map(
        local, mesh=mesh, in_specs=placed, out_specs=P(("dp", "expert"), None), check_vma=False
    )
```
